32 devices in a mesh: view: 8 (over y, x, core), walk: 4 (over z).
Axes of the slice: x: 2, y: 2, z: 4, core: 2. Of those that a mesh axis runs over, the one named last changes fastest.
Arguments:
- positions: float32 [64, 1024], P('walk', 'view'), may hold values from -21 to 21
- tile_values: bfloat16 [512, 128, 128], P('view'), may hold values from -0.25 to 0.25
- tile_rays: int32 [512], P('view'), may hold values from 0 to 15, as said below
- tile_voxels: int32 [512], P('view'), may hold values from 0 to 7
- tile_count: int32 [8], P('view'), may hold values from 16 to 64, as said below
- measured: float32 [16384], P('view'), may hold values from -6 to 6
- langevin_noise: float32 [64, 64], P('walk'), may hold values from -6 to 6
Outputs:
- gradient: float32 [64, 1024], P('walk', 'view')
- displacement: float32 [64, 1024], P('walk', 'view')
The draws below stay inside these ranges and needn't reach their ends.
Inputs may be any that keep to these rules, and one draw needn't show every extreme that they name: `tile_rays`: the 64 slots of one view index name distinct pairs of ray block and voxel block, live slots or not. The live slots of a view index are its first tile_count slots; some view index has all 64 live.
All inputs are finite; a program needn't handle non-finite values.
Results may differ from the reference program's by a relative error of at most 0.0029.
Values may be sent and summed in bfloat16 or wider, within the bound.
A program may use at most 64 MiB of HBM per device.

```python
import math
import jax
import jax.numpy as jnp
from jax import lax

TILE = 128
VOX_DEV = 128
RBLK_DEV = 16
TILES_CAP = 64
WALKERS = 64
NVOX = 1024
VBLK = 8
RAYS = 16384
TILES = 512


def tile_pairs(key):
    view_count = NVOX // VOX_DEV
    keys = jax.random.split(jax.random.fold_in(key, 11), view_count)
    chosen = jax.vmap(lambda single: jax.random.permutation(single, RBLK_DEV * VBLK)[:TILES_CAP])(keys)
    return chosen.reshape(-1).astype(jnp.int32)


def draw_tile_rays(key, part):
    return (tile_pairs(key) // VBLK).astype(jnp.int32)


def draw_tile_voxels(key, part):
    return (tile_pairs(key) % VBLK).astype(jnp.int32)


def draw_tile_count(key, part):
    view_count = NVOX // VOX_DEV
    first_key = jax.random.fold_in(key, 23)
    second_key = jax.random.fold_in(key, 29)
    counts = jax.random.randint(first_key, (view_count,), TILES_CAP // 4, TILES_CAP + 1)
    fullest = jax.random.randint(second_key, (), 0, view_count)
    counts = jnp.where(jnp.arange(view_count, dtype=jnp.int32) == fullest, TILES_CAP, counts)
    return counts.astype(jnp.int32)


def draw_positions(key, part):
    keys = jax.random.split(key, 3)
    columns = jnp.arange(NVOX, dtype=jnp.float32)
    ramp = 1.0 + 2.0 * columns / max(NVOX - 1, 1)
    column_scale = jnp.exp(jax.random.uniform(keys[1], (NVOX,), jnp.float32, math.log(0.3), math.log(3.0))) * ramp * 0.08
    row_scale = jnp.exp(jax.random.uniform(keys[2], (WALKERS, 1), jnp.float32, math.log(0.3), math.log(3.0)))
    base_values = jnp.clip(jax.random.normal(keys[0], (WALKERS, NVOX), jnp.float32), -4.0, 4.0)
    values = base_values * row_scale * column_scale[None, :]
    values = jnp.clip(values, -21.0, 21.0)
    return values.astype(jnp.float32)


def level_of(rng, shape, shards, low, largest):
    gain = 1.0
    for position, parts in shards:
        steps = jax.random.uniform(jax.random.fold_in(jax.random.fold_in(rng, 6), position), (parts,), jnp.float32, low / len(shards), largest / len(shards))
        gain = gain * jnp.repeat(jnp.exp(steps), shape[position] // parts).reshape((-1,) + (1,) * (len(shape) - 1 - position))
    return gain


def centred(stream_key, extent, spread, limit, cuts=(), kind=jnp.bfloat16):
    loudness = level_of(stream_key, extent, cuts, -0.22, 0.18) if cuts else 1.0
    result = jax.random.normal(stream_key, extent, jnp.float32) * spread * loudness
    return jnp.minimum(jnp.maximum(result, -limit), limit).astype(kind)


def setup_inputs(seed: int = 0) -> dict:
    seeds = jax.random.split(jax.random.key(seed), 8)
    return {
        "positions": draw_positions(jax.random.fold_in(seeds[7], 71), 0),
        "tile_values": centred(seeds[1], (TILES, TILE, TILE), (TILE * TILES_CAP // RBLK_DEV) ** -0.5, 0.25, ((0, 8),)),
        "tile_rays": draw_tile_rays(jax.random.fold_in(seeds[7], 71), 0),
        "tile_voxels": draw_tile_voxels(jax.random.fold_in(seeds[7], 71), 0),
        "tile_count": draw_tile_count(jax.random.fold_in(seeds[7], 71), 0),
        "measured": centred(seeds[5], (RAYS,), 1.0, 6.0, ((0, 8),), jnp.float32),
        "langevin_noise": centred(seeds[6], (WALKERS, WALKERS), 1.0, 6.0, ((0, 4),), jnp.float32),
    }


def reference(positions, tile_values, tile_rays, tile_voxels, tile_count, measured, langevin_noise):
    walkers, voxel_count = positions.shape
    view_count = tile_count.shape[0]
    slot_count = tile_values.shape[0] // view_count
    tile_size = tile_values.shape[1]
    voxel_blocks = voxel_count // tile_size
    ray_blocks = measured.shape[0] // (view_count * tile_size)
    rounded = lax.optimization_barrier(positions.astype(jnp.bfloat16))
    blocks = rounded.astype(jnp.float32).reshape(walkers, voxel_blocks, tile_size)
    tile_sets = tile_values.reshape(view_count, slot_count, tile_size, tile_size)
    ray_table = tile_rays.reshape(view_count, slot_count)
    voxel_table = tile_voxels.reshape(view_count, slot_count)
    observed = measured.reshape(view_count, ray_blocks, tile_size)
    live_table = (jnp.arange(slot_count, dtype=jnp.int32)[None, :] < tile_count[:, None]).astype(jnp.float32)

    def one_view(backprojected, inputs):
        values, ray_ids, vox_ids, live_mask, observed_rows = inputs
        values_wide = values.astype(jnp.float32)
        picked = blocks[:, vox_ids]
        product = jnp.einsum('gri,jgi->gjr', values_wide, picked, precision=lax.Precision.HIGHEST)
        product = product * live_mask[:, None, None]
        projected = jnp.zeros((ray_blocks, walkers, tile_size), jnp.float32).at[ray_ids].add(product)
        residual = lax.optimization_barrier((projected - observed_rows[:, None, :]).astype(jnp.bfloat16))
        ray_picked = residual.astype(jnp.float32)[ray_ids]
        contribution = jnp.einsum('gri,gjr->gji', values_wide, ray_picked, precision=lax.Precision.HIGHEST)
        contribution = contribution * live_mask[:, None, None]
        return (backprojected.at[vox_ids].add(contribution), None)
    start_value = jnp.zeros((voxel_blocks, walkers, tile_size), jnp.float32)
    backprojected, unused = lax.scan(one_view, start_value, (tile_sets, ray_table, voxel_table, live_table, observed))
    backprojected = jnp.transpose(backprojected, (1, 0, 2)).reshape(walkers, voxel_count)
    gradient = 4.0 * backprojected + positions
    ensemble_mean = lax.optimization_barrier(jnp.mean(positions, axis=0))
    deviation = positions - ensemble_mean[None, :]
    gram_matrix = jnp.dot(deviation, gradient.T, precision=lax.Precision.HIGHEST)
    step_size = walkers / (4.0 * (voxel_count + 1))
    coefficient = -(step_size / walkers) * gram_matrix + jnp.sqrt(2.0 * step_size / walkers) * langevin_noise.T
    displacement = jnp.dot(coefficient.T, deviation, precision=lax.Precision.HIGHEST)
    displacement = displacement + step_size * (voxel_count + 1) / walkers * deviation
    return (gradient, displacement)
```

```python
import functools
import math

import jax
import jax.numpy as jnp
from jax import lax
from jax.experimental import pallas as pl
from jax.experimental.pallas import tpu as pltpu
from jax.sharding import PartitionSpec as P

misfit_weight = 4.0
MESH = pl.DeviceIdType.MESH
GROUP = 8
CHUNKS = 4


def each(start, stop, body):
    if stop - start <= 16:
        for index in range(start, stop):
            body(index)
    else:

        @pl.loop(start, stop)
        def _(index):
            body(index)


def split_high_low(value):
    high = value.astype(jnp.bfloat16)
    low = (value - high.astype(jnp.float32)).astype(jnp.bfloat16)
    return high, low


def dot_t(left, right, precision=None):
    return lax.dot_general(
        left,
        right,
        (((1,), (1,)), ((), ())),
        precision=precision,
        preferred_element_type=jnp.float32,
    )


def step_kernel(
    views,
    walks,
    pos_ref,
    tiles_hbm,
    rays_ref,
    voxels_ref,
    count_ref,
    measured_ref,
    noise_ref,
    grad_ref,
    disp_ref,
    tiles,
    xpad,
    rpad,
    ens,
    devs,
    back,
    brecv,
    grecv,
    acc_f,
    tile_sem,
    x_send,
    x_recv,
    w_send,
    w_recv,
    d_send,
    d_recv,
    b_send,
    b_recv,
    g_send,
    g_recv,
):
    me_v = lax.axis_index("view")
    me_w = lax.axis_index("walk")
    rows = pos_ref.shape[0]
    slots, tile, _ = tiles.shape
    ray_blocks = measured_ref.shape[0]
    walkers = rows * walks
    voxel_count = views * tile
    chunk = slots // CHUNKS

    barrier = pltpu.get_barrier_semaphore()

    def greet_view(d):
        pl.semaphore_signal(
            barrier,
            inc=1,
            device_id={"view": lax.rem(me_v + d, views)},
            device_id_type=MESH,
        )

    def greet_walk(d):
        pl.semaphore_signal(
            barrier,
            inc=1,
            device_id={"walk": lax.rem(me_w + d, walks)},
            device_id_type=MESH,
        )

    each(1, walks, greet_walk)
    each(1, views, greet_view)

    def tile_copy(c):
        part = pl.ds(c * chunk, chunk)
        return pltpu.make_async_copy(tiles_hbm.at[part], tiles.at[part], tile_sem.at[c])

    for c in range(CHUNKS):
        tile_copy(c).start()

    positions = pos_ref[...]
    xpad[me_v, ray_blocks] = positions.astype(jnp.bfloat16)
    ens[me_w] = positions

    pl.semaphore_wait(barrier, views + walks - 2)

    def view_copy(d, src, dst, send, recv):
        return pltpu.make_async_remote_copy(
            src_ref=src,
            dst_ref=dst,
            send_sem=send.at[d],
            recv_sem=recv.at[d],
            device_id={"view": lax.rem(me_v + d, views)},
            device_id_type=MESH,
        )

    def origin(d):
        return lax.rem(me_v - d + views, views)

    def x_copy(d, owner):
        part = xpad.at[owner, ray_blocks]
        return view_copy(d, part, part, x_send, x_recv)

    def w_copy(d, owner):
        return pltpu.make_async_remote_copy(
            src_ref=ens.at[owner],
            dst_ref=ens.at[owner],
            send_sem=w_send.at[d],
            recv_sem=w_recv.at[d],
            device_id={"walk": lax.rem(me_w + d, walks)},
            device_id_type=MESH,
        )

    def d_copy(d, owner):
        return view_copy(d, devs.at[owner], devs.at[owner], d_send, d_recv)

    def b_copy(d, source, owner):
        return view_copy(d, back.at[source], brecv.at[owner], b_send, b_recv)

    def g_copy(d, owner):
        return view_copy(d, grecv.at[owner], grecv.at[owner], g_send, g_recv)

    each(1, views, lambda d: x_copy(d, me_v).start())
    each(1, walks, lambda d: w_copy(d, me_w).start())

    def clear(ref, index, middle):
        size = ref.shape[1]
        after = size - middle - 1
        ref[index, pl.ds(0, middle)] = jnp.zeros((middle, rows, tile), jnp.bfloat16)
        ref[index, pl.ds(middle + 1, after)] = jnp.zeros((after, rows, tile), jnp.bfloat16)

    each(0, views, lambda v: clear(xpad, v, ray_blocks))
    each(0, ray_blocks, lambda b: clear(rpad, b, views))

    each(1, walks, lambda d: w_copy(d, lax.rem(me_w - d + walks, walks)).wait_recv())
    ensemble = ens[...].reshape(walkers, tile)
    mean = jnp.sum(ensemble, axis=0, keepdims=True) / walkers
    deviation = ensemble - mean
    devs[me_v] = deviation.astype(jnp.bfloat16)
    each(1, views, lambda d: d_copy(d, me_v).start())
    own_gram = dot_t(positions, deviation, lax.Precision.HIGHEST)

    live = count_ref[0]

    def is_live(s):
        return jnp.minimum(jnp.maximum(live - s, 0), 1)

    each(1, views, lambda d: x_copy(d, origin(d)).wait_recv())
    for c in range(CHUNKS):
        tile_copy(c).wait()

    def forward_group(first):
        lefts, rights = [], []
        for k in range(GROUP):
            s = first + k
            start = is_live(s) * (ray_blocks - rays_ref[s])
            window = xpad[voxels_ref[s], pl.ds(start, ray_blocks)]
            lefts.append(window.reshape(ray_blocks * rows, tile))
            rights.append(tiles[s])
        return dot_t(jnp.concatenate(lefts, axis=1), jnp.concatenate(rights, axis=1))

    def adjoint_group(first):
        lefts = []
        for k in range(GROUP):
            s = first + k
            start = is_live(s) * (views - voxels_ref[s])
            window = rpad[rays_ref[s], pl.ds(start, views)]
            lefts.append(window.reshape(views * rows, tile))
        right = tiles[pl.ds(first, GROUP)].reshape(GROUP * tile, tile)
        return jnp.dot(
            jnp.concatenate(lefts, axis=1), right, preferred_element_type=jnp.float32
        )

    def total(group, window, store):
        if window * rows <= 512:
            value = group(0)
            for first in range(GROUP, slots, GROUP):
                value = value + group(first)
            store[...] = value.reshape(store.shape)
        else:
            store[...] = jnp.zeros_like(store)

            @pl.loop(0, slots // GROUP)
            def _(g):
                store[...] += group(g * GROUP).reshape(store.shape)

    total(forward_group, ray_blocks, acc_f)
    for b in range(ray_blocks):
        residual = acc_f[b] - measured_ref[pl.ds(b, 1), :]
        rpad[b, views] = residual.astype(jnp.bfloat16)
    total(adjoint_group, views, back)

    each(1, views, lambda d: b_copy(d, lax.rem(me_v + d, views), me_v).start())
    brecv[me_v] = back[me_v]

    each(1, views, lambda d: d_copy(d, origin(d)).wait_recv())
    if views <= 16:
        wide = jnp.concatenate([back[v] for v in range(views)], axis=1)
        spread = jnp.concatenate([devs[v] for v in range(views)], axis=1)
        high, low = split_high_low(wide)
        gram = dot_t(high, spread) + dot_t(low, spread)
    else:

        def add(v, gram):
            high, low = split_high_low(back[v])
            return gram + dot_t(high, devs[v]) + dot_t(low, devs[v])

        gram = lax.fori_loop(0, views, add, jnp.zeros((rows, walkers), jnp.float32))
    grecv[me_v] = misfit_weight * gram + own_gram
    each(1, views, lambda d: g_copy(d, me_v).start())

    each(1, views, lambda d: b_copy(d, 0, origin(d)).wait_recv())
    grad_ref[...] = misfit_weight * jnp.sum(brecv[...], axis=0) + positions

    each(1, views, lambda d: g_copy(d, origin(d)).wait_recv())
    gram = jnp.sum(grecv[...], axis=0)
    step_size = walkers / (4.0 * (voxel_count + 1))
    coefficient = (
        -(step_size / walkers) * gram
        + math.sqrt(2.0 * step_size / walkers) * noise_ref[...]
    )
    moved = jnp.dot(
        coefficient,
        deviation,
        precision=lax.Precision.HIGHEST,
        preferred_element_type=jnp.float32,
    )
    own_deviation = positions - mean
    disp_ref[...] = moved + step_size * (voxel_count + 1) / walkers * own_deviation

    each(1, walks, lambda d: w_copy(d, me_w).wait_send())

    def drain(d):
        x_copy(d, me_v).wait_send()
        d_copy(d, me_v).wait_send()
        b_copy(d, 0, me_v).wait_send()
        g_copy(d, me_v).wait_send()

    each(1, views, drain)


def shards(views, walks, positions, tile_values, tile_rays, tile_voxels, tile_count, measured, langevin_noise):
    rows, tile = positions.shape
    slots = tile_values.shape[0]
    ray_blocks = measured.shape[0] // tile
    walkers = rows * walks
    dma = pltpu.SemaphoreType.DMA
    vmem = pl.BlockSpec(memory_space=pltpu.VMEM)
    smem = pl.BlockSpec(memory_space=pltpu.SMEM)
    out = jax.ShapeDtypeStruct((rows, tile), jnp.float32)
    return pl.pallas_call(
        functools.partial(step_kernel, views, walks),
        out_shape=(out, out),
        in_specs=[
            vmem,
            pl.BlockSpec(memory_space=pl.ANY),
            smem,
            smem,
            smem,
            vmem,
            vmem,
        ],
        out_specs=(vmem, vmem),
        scratch_shapes=[
            pltpu.VMEM((slots, tile, tile), jnp.bfloat16),
            pltpu.VMEM((views, 2 * ray_blocks, rows, tile), jnp.bfloat16),
            pltpu.VMEM((ray_blocks, 2 * views, rows, tile), jnp.bfloat16),
            pltpu.VMEM((walks, rows, tile), jnp.float32),
            pltpu.VMEM((views, walkers, tile), jnp.bfloat16),
            pltpu.VMEM((views, rows, tile), jnp.float32),
            pltpu.VMEM((views, rows, tile), jnp.float32),
            pltpu.VMEM((views, rows, walkers), jnp.float32),
            pltpu.VMEM((ray_blocks, rows, tile), jnp.float32),
            dma((CHUNKS,)),
            dma((views,)),
            dma((views,)),
            dma((walks,)),
            dma((walks,)),
            dma((views,)),
            dma((views,)),
            dma((views,)),
            dma((views,)),
            dma((views,)),
            dma((views,)),
        ],
        compiler_params=pltpu.CompilerParams(
            collective_id=0,
            has_side_effects=True,
            vmem_limit_bytes=56 * 1024 * 1024,
        ),
        cost_estimate=pl.CostEstimate(
            flops=4 * slots * tile * tile * rows,
            bytes_accessed=2 * slots * tile * tile,
            transcendentals=0,
        ),
    )(
        positions,
        tile_values,
        tile_rays,
        tile_voxels,
        tile_count,
        measured.reshape(ray_blocks, tile),
        langevin_noise,
    )


def solution(mesh):
    in_specs = (
        P("walk", "view"),
        P("view", None, None),
        P("view"),
        P("view"),
        P("view"),
        P("view"),
        P("walk", None),
    )
    out_specs = (P("walk", "view"), P("walk", "view"))
    body = functools.partial(shards, mesh.shape["view"], mesh.shape["walk"])
    return jax.shard_map(body, mesh=mesh, in_specs=in_specs, out_specs=out_specs, check_vma=False)
```

```python
import functools
import math

import jax
import jax.numpy as jnp
from jax import lax
from jax.experimental import pallas as pl
from jax.experimental.pallas import tpu as pltpu
from jax.sharding import PartitionSpec as P

misfit_weight = 4.0
MESH = pl.DeviceIdType.MESH
GROUP = 8
CHUNKS = 4


def each(start, stop, body):
    if stop - start <= 16:
        for index in range(start, stop):
            body(index)
    else:

        @pl.loop(start, stop)
        def _(index):
            body(index)


def split_high_low(value):
    high = value.astype(jnp.bfloat16)
    low = (value - high.astype(jnp.float32)).astype(jnp.bfloat16)
    return high, low


def dot_t(left, right, precision=None):
    return lax.dot_general(
        left,
        right,
        (((1,), (1,)), ((), ())),
        precision=precision,
        preferred_element_type=jnp.float32,
    )


def step_kernel(
    views,
    walks,
    pos_ref,
    tiles_hbm,
    rays_hbm,
    voxels_hbm,
    count_hbm,
    measured_hbm,
    noise_hbm,
    grad_ref,
    disp_ref,
    rays_ref,
    voxels_ref,
    count_ref,
    measured_ref,
    noise_ref,
    small_sem,
    tiles,
    xpad,
    rpad,
    ens,
    devs,
    back,
    brecv,
    grecv,
    acc_f,
    tile_sem,
    x_send,
    x_recv,
    w_send,
    w_recv,
    d_send,
    d_recv,
    b_send,
    b_recv,
    g_send,
    g_recv,
):
    me_v = lax.axis_index("view")
    me_w = lax.axis_index("walk")
    rows = pos_ref.shape[0]
    slots, tile, _ = tiles.shape
    ray_blocks = measured_ref.shape[0]
    walkers = rows * walks
    voxel_count = views * tile
    chunk = slots // CHUNKS

    barrier = pltpu.get_barrier_semaphore()

    def greet_view(d):
        pl.semaphore_signal(
            barrier,
            inc=1,
            device_id={"view": lax.rem(me_v + d, views)},
            device_id_type=MESH,
        )

    def greet_walk(d):
        pl.semaphore_signal(
            barrier,
            inc=1,
            device_id={"walk": lax.rem(me_w + d, walks)},
            device_id_type=MESH,
        )

    each(1, walks, greet_walk)
    each(1, views, greet_view)

    def tile_copy(c):
        part = pl.ds(c * chunk, chunk)
        return pltpu.make_async_copy(tiles_hbm.at[part], tiles.at[part], tile_sem.at[c])

    small = [
        pltpu.make_async_copy(source, target, small_sem.at[k])
        for k, (source, target) in enumerate(
            (
                (rays_hbm, rays_ref),
                (voxels_hbm, voxels_ref),
                (count_hbm, count_ref),
                (measured_hbm, measured_ref),
                (noise_hbm, noise_ref),
            )
        )
    ]
    for copy in small:
        copy.start()
    for c in range(CHUNKS):
        tile_copy(c).start()

    positions = pos_ref[...]
    xpad[me_v, ray_blocks] = positions.astype(jnp.bfloat16)
    ens[me_w] = positions

    pl.semaphore_wait(barrier, views + walks - 2)

    def view_copy(d, src, dst, send, recv):
        return pltpu.make_async_remote_copy(
            src_ref=src,
            dst_ref=dst,
            send_sem=send.at[d],
            recv_sem=recv.at[d],
            device_id={"view": lax.rem(me_v + d, views)},
            device_id_type=MESH,
        )

    def origin(d):
        return lax.rem(me_v - d + views, views)

    def x_copy(d, owner):
        part = xpad.at[owner, ray_blocks]
        return view_copy(d, part, part, x_send, x_recv)

    def w_copy(d, owner):
        return pltpu.make_async_remote_copy(
            src_ref=ens.at[owner],
            dst_ref=ens.at[owner],
            send_sem=w_send.at[d],
            recv_sem=w_recv.at[d],
            device_id={"walk": lax.rem(me_w + d, walks)},
            device_id_type=MESH,
        )

    def d_copy(d, owner):
        return view_copy(d, devs.at[owner], devs.at[owner], d_send, d_recv)

    def b_copy(d, source, owner):
        return view_copy(d, back.at[source], brecv.at[owner], b_send, b_recv)

    def g_copy(d, owner):
        return view_copy(d, grecv.at[owner], grecv.at[owner], g_send, g_recv)

    each(1, views, lambda d: x_copy(d, me_v).start())
    each(1, walks, lambda d: w_copy(d, me_w).start())

    def clear(ref, index, middle):
        size = ref.shape[1]
        after = size - middle - 1
        ref[index, pl.ds(0, middle)] = jnp.zeros((middle, rows, tile), jnp.bfloat16)
        ref[index, pl.ds(middle + 1, after)] = jnp.zeros((after, rows, tile), jnp.bfloat16)

    each(0, views, lambda v: clear(xpad, v, ray_blocks))
    each(0, ray_blocks, lambda b: clear(rpad, b, views))

    each(1, walks, lambda d: w_copy(d, lax.rem(me_w - d + walks, walks)).wait_recv())
    ensemble = ens[...].reshape(walkers, tile)
    mean = jnp.sum(ensemble, axis=0, keepdims=True) / walkers
    deviation = ensemble - mean
    devs[me_v] = deviation.astype(jnp.bfloat16)
    each(1, views, lambda d: d_copy(d, me_v).start())
    own_gram = dot_t(positions, deviation, lax.Precision.HIGHEST)

    for copy in small:
        copy.wait()
    live = count_ref[0]

    def is_live(s):
        return jnp.minimum(jnp.maximum(live - s, 0), 1)

    each(1, views, lambda d: x_copy(d, origin(d)).wait_recv())
    for c in range(CHUNKS):
        tile_copy(c).wait()

    def forward_group(first):
        lefts, rights = [], []
        for k in range(GROUP):
            s = first + k
            start = is_live(s) * (ray_blocks - rays_ref[s])
            window = xpad[voxels_ref[s], pl.ds(start, ray_blocks)]
            lefts.append(window.reshape(ray_blocks * rows, tile))
            rights.append(tiles[s])
        return dot_t(jnp.concatenate(lefts, axis=1), jnp.concatenate(rights, axis=1))

    def adjoint_group(first):
        lefts = []
        for k in range(GROUP):
            s = first + k
            start = is_live(s) * (views - voxels_ref[s])
            window = rpad[rays_ref[s], pl.ds(start, views)]
            lefts.append(window.reshape(views * rows, tile))
        right = tiles[pl.ds(first, GROUP)].reshape(GROUP * tile, tile)
        return jnp.dot(
            jnp.concatenate(lefts, axis=1), right, preferred_element_type=jnp.float32
        )

    def total(group, window, store):
        if window * rows <= 512:
            value = group(0)
            for first in range(GROUP, slots, GROUP):
                value = value + group(first)
            store[...] = value.reshape(store.shape)
        else:
            store[...] = jnp.zeros_like(store)

            @pl.loop(0, slots // GROUP)
            def _(g):
                store[...] += group(g * GROUP).reshape(store.shape)

    total(forward_group, ray_blocks, acc_f)
    for b in range(ray_blocks):
        residual = acc_f[b] - measured_ref[pl.ds(b, 1), :]
        rpad[b, views] = residual.astype(jnp.bfloat16)
    total(adjoint_group, views, back)

    each(1, views, lambda d: b_copy(d, lax.rem(me_v + d, views), me_v).start())
    brecv[me_v] = back[me_v]

    each(1, views, lambda d: d_copy(d, origin(d)).wait_recv())
    if views <= 16:
        wide = jnp.concatenate([back[v] for v in range(views)], axis=1)
        spread = jnp.concatenate([devs[v] for v in range(views)], axis=1)
        high, low = split_high_low(wide)
        gram = dot_t(high, spread) + dot_t(low, spread)
    else:

        def add(v, gram):
            high, low = split_high_low(back[v])
            return gram + dot_t(high, devs[v]) + dot_t(low, devs[v])

        gram = lax.fori_loop(0, views, add, jnp.zeros((rows, walkers), jnp.float32))
    grecv[me_v] = misfit_weight * gram + own_gram
    each(1, views, lambda d: g_copy(d, me_v).start())

    each(1, views, lambda d: b_copy(d, 0, origin(d)).wait_recv())
    grad_ref[...] = misfit_weight * jnp.sum(brecv[...], axis=0) + positions

    each(1, views, lambda d: g_copy(d, origin(d)).wait_recv())
    gram = jnp.sum(grecv[...], axis=0)
    step_size = walkers / (4.0 * (voxel_count + 1))
    coefficient = (
        -(step_size / walkers) * gram
        + math.sqrt(2.0 * step_size / walkers) * noise_ref[...]
    )
    moved = jnp.dot(
        coefficient,
        deviation,
        precision=lax.Precision.HIGHEST,
        preferred_element_type=jnp.float32,
    )
    own_deviation = positions - mean
    disp_ref[...] = moved + step_size * (voxel_count + 1) / walkers * own_deviation

    each(1, walks, lambda d: w_copy(d, me_w).wait_send())

    def drain(d):
        x_copy(d, me_v).wait_send()
        d_copy(d, me_v).wait_send()
        b_copy(d, 0, me_v).wait_send()
        g_copy(d, me_v).wait_send()

    each(1, views, drain)


def shards(views, walks, positions, tile_values, tile_rays, tile_voxels, tile_count, measured, langevin_noise):
    rows, tile = positions.shape
    slots = tile_values.shape[0]
    ray_blocks = measured.shape[0] // tile
    walkers = rows * walks
    dma = pltpu.SemaphoreType.DMA
    vmem = pl.BlockSpec(memory_space=pltpu.VMEM)
    hbm = pl.BlockSpec(memory_space=pltpu.HBM)
    held = pltpu.VMEM((rows, tile), jnp.float32)
    gradient, displacement = pl.pallas_call(
        functools.partial(step_kernel, views, walks),
        out_shape=(held, held),
        in_specs=[vmem, hbm, hbm, hbm, hbm, hbm, hbm],
        out_specs=(vmem, vmem),
        scratch_shapes=[
            pltpu.SMEM(tile_rays.shape, jnp.int32),
            pltpu.SMEM(tile_voxels.shape, jnp.int32),
            pltpu.SMEM(tile_count.shape, jnp.int32),
            pltpu.VMEM((ray_blocks, tile), jnp.float32),
            pltpu.VMEM(langevin_noise.shape, jnp.float32),
            dma((5,)),
            pltpu.VMEM((slots, tile, tile), jnp.bfloat16),
            pltpu.VMEM((views, 2 * ray_blocks, rows, tile), jnp.bfloat16),
            pltpu.VMEM((ray_blocks, 2 * views, rows, tile), jnp.bfloat16),
            pltpu.VMEM((walks, rows, tile), jnp.float32),
            pltpu.VMEM((views, walkers, tile), jnp.bfloat16),
            pltpu.VMEM((views, rows, tile), jnp.float32),
            pltpu.VMEM((views, rows, tile), jnp.float32),
            pltpu.VMEM((views, rows, walkers), jnp.float32),
            pltpu.VMEM((ray_blocks, rows, tile), jnp.float32),
            dma((CHUNKS,)),
            dma((views,)),
            dma((views,)),
            dma((walks,)),
            dma((walks,)),
            dma((views,)),
            dma((views,)),
            dma((views,)),
            dma((views,)),
            dma((views,)),
            dma((views,)),
        ],
        compiler_params=pltpu.CompilerParams(
            collective_id=0,
            has_side_effects=True,
            vmem_limit_bytes=56 * 1024 * 1024,
        ),
        cost_estimate=pl.CostEstimate(
            flops=4 * slots * tile * tile * rows,
            bytes_accessed=2 * slots * tile * tile,
            transcendentals=0,
        ),
    )(
        positions,
        tile_values,
        tile_rays,
        tile_voxels,
        tile_count,
        measured.reshape(ray_blocks, tile),
        langevin_noise,
    )
    return gradient, displacement


def solution(mesh):
    in_specs = (
        P("walk", "view"),
        P("view", None, None),
        P("view"),
        P("view"),
        P("view"),
        P("view"),
        P("walk", None),
    )
    out_specs = (P("walk", "view"), P("walk", "view"))
    body = functools.partial(shards, mesh.shape["view"], mesh.shape["walk"])
    return jax.shard_map(body, mesh=mesh, in_specs=in_specs, out_specs=out_specs, check_vma=False)
```

```python
import functools
import math

import jax
import jax.numpy as jnp
from jax import lax
from jax.experimental import pallas as pl
from jax.experimental.pallas import tpu as pltpu
from jax.sharding import PartitionSpec as P

misfit_weight = 4.0
MESH = pl.DeviceIdType.MESH
GROUP = 8
CHUNKS = 4


def each(start, stop, body):
    if stop - start <= 16:
        for index in range(start, stop):
            body(index)
    else:

        @pl.loop(start, stop)
        def _(index):
            body(index)


def split_high_low(value):
    high = value.astype(jnp.bfloat16)
    low = (value - high.astype(jnp.float32)).astype(jnp.bfloat16)
    return high, low


def dot_t(left, right, precision=None):
    return lax.dot_general(
        left,
        right,
        (((1,), (1,)), ((), ())),
        precision=precision,
        preferred_element_type=jnp.float32,
    )


def step_kernel(
    views,
    walks,
    pos_ref,
    tiles_hbm,
    rays_hbm,
    voxels_hbm,
    count_hbm,
    measured_hbm,
    noise_hbm,
    out_ref,
    rays_ref,
    voxels_ref,
    count_ref,
    measured_ref,
    noise_ref,
    small_sem,
    tiles,
    xpad,
    rpad,
    ens,
    devs,
    back,
    brecv,
    grecv,
    acc_f,
    tile_sem,
    x_send,
    x_recv,
    w_send,
    w_recv,
    d_send,
    d_recv,
    b_send,
    b_recv,
    g_send,
    g_recv,
):
    me_v = lax.axis_index("view")
    me_w = lax.axis_index("walk")
    rows = pos_ref.shape[0]
    slots, tile, _ = tiles.shape
    ray_blocks = measured_ref.shape[0]
    walkers = rows * walks
    voxel_count = views * tile
    chunk = slots // CHUNKS

    barrier = pltpu.get_barrier_semaphore()

    def greet_view(d):
        pl.semaphore_signal(
            barrier,
            inc=1,
            device_id={"view": lax.rem(me_v + d, views)},
            device_id_type=MESH,
        )

    def greet_walk(d):
        pl.semaphore_signal(
            barrier,
            inc=1,
            device_id={"walk": lax.rem(me_w + d, walks)},
            device_id_type=MESH,
        )

    each(1, walks, greet_walk)
    each(1, views, greet_view)

    def tile_copy(c):
        part = pl.ds(c * chunk, chunk)
        return pltpu.make_async_copy(tiles_hbm.at[part], tiles.at[part], tile_sem.at[c])

    small = [
        pltpu.make_async_copy(source, target, small_sem.at[k])
        for k, (source, target) in enumerate(
            (
                (rays_hbm, rays_ref),
                (voxels_hbm, voxels_ref),
                (count_hbm, count_ref),
                (measured_hbm, measured_ref),
                (noise_hbm, noise_ref),
            )
        )
    ]
    for copy in small:
        copy.start()
    for c in range(CHUNKS):
        tile_copy(c).start()

    positions = pos_ref[...]
    xpad[me_v, ray_blocks] = positions.astype(jnp.bfloat16)
    ens[me_w] = positions

    pl.semaphore_wait(barrier, views + walks - 2)

    def view_copy(d, src, dst, send, recv):
        return pltpu.make_async_remote_copy(
            src_ref=src,
            dst_ref=dst,
            send_sem=send.at[d],
            recv_sem=recv.at[d],
            device_id={"view": lax.rem(me_v + d, views)},
            device_id_type=MESH,
        )

    def origin(d):
        return lax.rem(me_v - d + views, views)

    def x_copy(d, owner):
        part = xpad.at[owner, ray_blocks]
        return view_copy(d, part, part, x_send, x_recv)

    def w_copy(d, owner):
        return pltpu.make_async_remote_copy(
            src_ref=ens.at[owner],
            dst_ref=ens.at[owner],
            send_sem=w_send.at[d],
            recv_sem=w_recv.at[d],
            device_id={"walk": lax.rem(me_w + d, walks)},
            device_id_type=MESH,
        )

    def d_copy(d, owner):
        return view_copy(d, devs.at[owner], devs.at[owner], d_send, d_recv)

    def b_copy(d, source, owner):
        return view_copy(d, back.at[source], brecv.at[owner], b_send, b_recv)

    def g_copy(d, owner):
        return view_copy(d, grecv.at[owner], grecv.at[owner], g_send, g_recv)

    each(1, walks, lambda d: w_copy(d, me_w).start())
    each(1, views, lambda d: x_copy(d, me_v).start())

    def clear(ref, index, middle):
        size = ref.shape[1]
        after = size - middle - 1
        ref[index, pl.ds(0, middle)] = jnp.zeros((middle, rows, tile), jnp.bfloat16)
        ref[index, pl.ds(middle + 1, after)] = jnp.zeros((after, rows, tile), jnp.bfloat16)

    each(0, views, lambda v: clear(xpad, v, ray_blocks))
    each(0, ray_blocks, lambda b: clear(rpad, b, views))

    each(1, walks, lambda d: w_copy(d, lax.rem(me_w - d + walks, walks)).wait_recv())
    ensemble = ens[...].reshape(walkers, tile)
    mean = jnp.sum(ensemble, axis=0, keepdims=True) / walkers
    deviation = ensemble - mean
    devs[me_v] = deviation.astype(jnp.bfloat16)
    each(1, views, lambda d: d_copy(d, me_v).start())

    for copy in small:
        copy.wait()
    live = count_ref[0]

    def is_live(s):
        return jnp.minimum(jnp.maximum(live - s, 0), 1)

    each(1, views, lambda d: x_copy(d, origin(d)).wait_recv())
    for c in range(CHUNKS):
        tile_copy(c).wait()

    def forward_group(first):
        lefts, rights = [], []
        for k in range(GROUP):
            s = first + k
            start = is_live(s) * (ray_blocks - rays_ref[s])
            window = xpad[voxels_ref[s], pl.ds(start, ray_blocks)]
            lefts.append(window.reshape(ray_blocks * rows, tile))
            rights.append(tiles[s])
        return dot_t(jnp.concatenate(lefts, axis=1), jnp.concatenate(rights, axis=1))

    def adjoint_group(first):
        lefts = []
        for k in range(GROUP):
            s = first + k
            start = is_live(s) * (views - voxels_ref[s])
            window = rpad[rays_ref[s], pl.ds(start, views)]
            lefts.append(window.reshape(views * rows, tile))
        right = tiles[pl.ds(first, GROUP)].reshape(GROUP * tile, tile)
        return jnp.dot(
            jnp.concatenate(lefts, axis=1), right, preferred_element_type=jnp.float32
        )

    def total(group, window, store):
        if window * rows <= 512:
            value = group(0)
            for first in range(GROUP, slots, GROUP):
                value = value + group(first)
            store[...] = value.reshape(store.shape)
        else:
            store[...] = jnp.zeros_like(store)

            @pl.loop(0, slots // GROUP)
            def _(g):
                store[...] += group(g * GROUP).reshape(store.shape)

    total(forward_group, ray_blocks, acc_f)
    for b in range(ray_blocks):
        residual = acc_f[b] - measured_ref[pl.ds(b, 1), :]
        rpad[b, views] = residual.astype(jnp.bfloat16)
    total(adjoint_group, views, back)

    each(1, views, lambda d: b_copy(d, lax.rem(me_v + d, views), me_v).start())
    brecv[me_v] = back[me_v]
    own_gram = dot_t(positions, deviation, lax.Precision.HIGHEST)

    each(1, views, lambda d: d_copy(d, origin(d)).wait_recv())
    if views <= 16:
        wide = jnp.concatenate([back[v] for v in range(views)], axis=1)
        spread = jnp.concatenate([devs[v] for v in range(views)], axis=1)
        high, low = split_high_low(wide)
        gram = dot_t(high, spread) + dot_t(low, spread)
    else:

        def add(v, gram):
            high, low = split_high_low(back[v])
            return gram + dot_t(high, devs[v]) + dot_t(low, devs[v])

        gram = lax.fori_loop(0, views, add, jnp.zeros((rows, walkers), jnp.float32))
    grecv[me_v] = misfit_weight * gram + own_gram
    each(1, views, lambda d: g_copy(d, me_v).start())

    def drain(d):
        x_copy(d, me_v).wait_send()
        d_copy(d, me_v).wait_send()
        b_copy(d, 0, me_v).wait_send()

    each(1, walks, lambda d: w_copy(d, me_w).wait_send())
    each(1, views, drain)

    each(1, views, lambda d: b_copy(d, 0, origin(d)).wait_recv())
    out_ref[0] = misfit_weight * jnp.sum(brecv[...], axis=0) + positions

    each(1, views, lambda d: g_copy(d, origin(d)).wait_recv())
    gram = jnp.sum(grecv[...], axis=0)
    step_size = walkers / (4.0 * (voxel_count + 1))
    coefficient = (
        -(step_size / walkers) * gram
        + math.sqrt(2.0 * step_size / walkers) * noise_ref[...]
    )
    moved = jnp.dot(
        coefficient,
        deviation,
        precision=lax.Precision.HIGHEST,
        preferred_element_type=jnp.float32,
    )
    own_deviation = positions - mean
    out_ref[1] = moved + step_size * (voxel_count + 1) / walkers * own_deviation

    each(1, views, lambda d: g_copy(d, me_v).wait_send())


def shards(views, walks, positions, tile_values, tile_rays, tile_voxels, tile_count, measured, langevin_noise):
    rows, tile = positions.shape
    slots = tile_values.shape[0]
    ray_blocks = measured.shape[0] // tile
    walkers = rows * walks
    dma = pltpu.SemaphoreType.DMA
    vmem = pl.BlockSpec(memory_space=pltpu.VMEM)
    hbm = pl.BlockSpec(memory_space=pltpu.HBM)
    both = pl.pallas_call(
        functools.partial(step_kernel, views, walks),
        out_shape=pltpu.VMEM((2, rows, tile), jnp.float32),
        in_specs=[vmem, hbm, hbm, hbm, hbm, hbm, hbm],
        out_specs=vmem,
        scratch_shapes=[
            pltpu.SMEM(tile_rays.shape, jnp.int32),
            pltpu.SMEM(tile_voxels.shape, jnp.int32),
            pltpu.SMEM(tile_count.shape, jnp.int32),
            pltpu.VMEM((ray_blocks, tile), jnp.float32),
            pltpu.VMEM(langevin_noise.shape, jnp.float32),
            dma((5,)),
            pltpu.VMEM((slots, tile, tile), jnp.bfloat16),
            pltpu.VMEM((views, 2 * ray_blocks, rows, tile), jnp.bfloat16),
            pltpu.VMEM((ray_blocks, 2 * views, rows, tile), jnp.bfloat16),
            pltpu.VMEM((walks, rows, tile), jnp.float32),
            pltpu.VMEM((views, walkers, tile), jnp.bfloat16),
            pltpu.VMEM((views, rows, tile), jnp.float32),
            pltpu.VMEM((views, rows, tile), jnp.float32),
            pltpu.VMEM((views, rows, walkers), jnp.float32),
            pltpu.VMEM((ray_blocks, rows, tile), jnp.float32),
            dma((CHUNKS,)),
            dma((views,)),
            dma((views,)),
            dma((walks,)),
            dma((walks,)),
            dma((views,)),
            dma((views,)),
            dma((views,)),
            dma((views,)),
            dma((views,)),
            dma((views,)),
        ],
        compiler_params=pltpu.CompilerParams(
            collective_id=0,
            has_side_effects=True,
            vmem_limit_bytes=56 * 1024 * 1024,
        ),
        cost_estimate=pl.CostEstimate(
            flops=4 * slots * tile * tile * rows,
            bytes_accessed=2 * slots * tile * tile,
            transcendentals=0,
        ),
    )(
        positions,
        tile_values,
        tile_rays,
        tile_voxels,
        tile_count,
        measured.reshape(ray_blocks, tile),
        langevin_noise,
    )
    return both[0], both[1]


def solution(mesh):
    in_specs = (
        P("walk", "view"),
        P("view", None, None),
        P("view"),
        P("view"),
        P("view"),
        P("view"),
        P("walk", None),
    )
    out_specs = (P("walk", "view"), P("walk", "view"))
    body = functools.partial(shards, mesh.shape["view"], mesh.shape["walk"])
    return jax.shard_map(body, mesh=mesh, in_specs=in_specs, out_specs=out_specs, check_vma=False)
```

```python
import functools
import math

import jax
import jax.numpy as jnp
from jax import lax
from jax.experimental import pallas as pl
from jax.experimental.pallas import tpu as pltpu
from jax.sharding import PartitionSpec as P

misfit_weight = 4.0
MESH = pl.DeviceIdType.MESH
GROUP = 8
CHUNKS = 4


def each(start, stop, body):
    if stop - start <= 16:
        for index in range(start, stop):
            body(index)
    else:

        @pl.loop(start, stop)
        def _(index):
            body(index)


def split_high_low(value):
    high = value.astype(jnp.bfloat16)
    low = (value - high.astype(jnp.float32)).astype(jnp.bfloat16)
    return high, low


def dot_t(left, right, precision=None):
    return lax.dot_general(
        left,
        right,
        (((1,), (1,)), ((), ())),
        precision=precision,
        preferred_element_type=jnp.float32,
    )


def step_kernel(
    views,
    walks,
    pos_ref,
    tiles_hbm,
    rays_hbm,
    voxels_hbm,
    count_hbm,
    measured_hbm,
    noise_hbm,
    out_ref,
    rays_ref,
    voxels_ref,
    count_ref,
    measured_ref,
    noise_ref,
    small_sem,
    tiles,
    xpad,
    rpad,
    ens,
    devs,
    back,
    brecv,
    grecv,
    acc_f,
    tile_sem,
    x_send,
    x_recv,
    w_send,
    w_recv,
    d_send,
    d_recv,
    b_send,
    b_recv,
    g_send,
    g_recv,
):
    me_v = lax.axis_index("view")
    me_w = lax.axis_index("walk")
    rows = pos_ref.shape[0]
    slots, tile, _ = tiles.shape
    ray_blocks = measured_ref.shape[0]
    walkers = rows * walks
    voxel_count = views * tile
    chunk = slots // CHUNKS

    barrier = pltpu.get_barrier_semaphore()

    def greet_view(d):
        pl.semaphore_signal(
            barrier,
            inc=1,
            device_id={"view": lax.rem(me_v + d, views)},
            device_id_type=MESH,
        )

    def greet_walk(d):
        pl.semaphore_signal(
            barrier,
            inc=1,
            device_id={"walk": lax.rem(me_w + d, walks)},
            device_id_type=MESH,
        )

    each(1, walks, greet_walk)
    each(1, views, greet_view)

    def tile_copy(c):
        part = pl.ds(c * chunk, chunk)
        return pltpu.make_async_copy(tiles_hbm.at[part], tiles.at[part], tile_sem.at[c])

    small = [
        pltpu.make_async_copy(source, target, small_sem.at[k])
        for k, (source, target) in enumerate(
            (
                (rays_hbm, rays_ref),
                (voxels_hbm, voxels_ref),
                (count_hbm, count_ref),
                (measured_hbm, measured_ref),
                (noise_hbm, noise_ref),
            )
        )
    ]
    for copy in small:
        copy.start()
    for c in range(CHUNKS):
        tile_copy(c).start()

    positions = pos_ref[...]
    xpad[me_v, ray_blocks] = positions.astype(jnp.bfloat16)
    ens[me_w] = positions

    pl.semaphore_wait(barrier, views + walks - 2)

    def view_copy(d, src, dst, send, recv):
        return pltpu.make_async_remote_copy(
            src_ref=src,
            dst_ref=dst,
            send_sem=send,
            recv_sem=recv,
            device_id={"view": lax.rem(me_v + d, views)},
            device_id_type=MESH,
        )

    def x_copy(d, owner):
        part = xpad.at[owner, ray_blocks]
        return view_copy(d, part, part, x_send, x_recv)

    def w_copy(d, owner):
        return pltpu.make_async_remote_copy(
            src_ref=ens.at[owner],
            dst_ref=ens.at[owner],
            send_sem=w_send,
            recv_sem=w_recv,
            device_id={"walk": lax.rem(me_w + d, walks)},
            device_id_type=MESH,
        )

    def d_copy(d, owner):
        return view_copy(d, devs.at[owner], devs.at[owner], d_send, d_recv)

    def b_copy(d, source, owner):
        return view_copy(d, back.at[source], brecv.at[owner], b_send, b_recv)

    def g_copy(d, owner):
        return view_copy(d, grecv.at[owner], grecv.at[owner], g_send, g_recv)

    def all_views(like, send, recv):
        return view_copy(1, like, like, send, recv)

    peers = pl.ds(0, views - 1)
    x_all = all_views(rpad.at[0, peers], x_send, x_recv)
    d_all = all_views(devs.at[peers], d_send, d_recv)
    b_all = all_views(brecv.at[peers], b_send, b_recv)
    g_all = all_views(grecv.at[peers], g_send, g_recv)
    w_part = ens.at[pl.ds(0, walks - 1)]
    w_all = pltpu.make_async_remote_copy(
        src_ref=w_part,
        dst_ref=w_part,
        send_sem=w_send,
        recv_sem=w_recv,
        device_id={"walk": lax.rem(me_w + 1, walks)},
        device_id_type=MESH,
    )

    each(1, walks, lambda d: w_copy(d, me_w).start())
    each(1, views, lambda d: x_copy(d, me_v).start())

    def clear(ref, index, middle):
        size = ref.shape[1]
        after = size - middle - 1
        ref[index, pl.ds(0, middle)] = jnp.zeros((middle, rows, tile), jnp.bfloat16)
        ref[index, pl.ds(middle + 1, after)] = jnp.zeros((after, rows, tile), jnp.bfloat16)

    each(0, views, lambda v: clear(xpad, v, ray_blocks))
    each(0, ray_blocks, lambda b: clear(rpad, b, views))

    w_all.wait_recv()
    ensemble = ens[...].reshape(walkers, tile)
    mean = jnp.sum(ensemble, axis=0, keepdims=True) / walkers
    deviation = ensemble - mean
    devs[me_v] = deviation.astype(jnp.bfloat16)
    each(1, views, lambda d: d_copy(d, me_v).start())

    for copy in small:
        copy.wait()
    live = count_ref[0]

    def is_live(s):
        return jnp.minimum(jnp.maximum(live - s, 0), 1)

    x_all.wait_recv()
    for c in range(CHUNKS):
        tile_copy(c).wait()

    def forward_group(first):
        lefts, rights = [], []
        for k in range(GROUP):
            s = first + k
            start = is_live(s) * (ray_blocks - rays_ref[s])
            window = xpad[voxels_ref[s], pl.ds(start, ray_blocks)]
            lefts.append(window.reshape(ray_blocks * rows, tile))
            rights.append(tiles[s])
        return dot_t(jnp.concatenate(lefts, axis=1), jnp.concatenate(rights, axis=1))

    def adjoint_group(first):
        lefts = []
        for k in range(GROUP):
            s = first + k
            start = is_live(s) * (views - voxels_ref[s])
            window = rpad[rays_ref[s], pl.ds(start, views)]
            lefts.append(window.reshape(views * rows, tile))
        right = tiles[pl.ds(first, GROUP)].reshape(GROUP * tile, tile)
        return jnp.dot(
            jnp.concatenate(lefts, axis=1), right, preferred_element_type=jnp.float32
        )

    def total(group, window, store):
        if window * rows <= 512:
            value = group(0)
            for first in range(GROUP, slots, GROUP):
                value = value + group(first)
            store[...] = value.reshape(store.shape)
        else:
            store[...] = jnp.zeros_like(store)

            @pl.loop(0, slots // GROUP)
            def _(g):
                store[...] += group(g * GROUP).reshape(store.shape)

    total(forward_group, ray_blocks, acc_f)
    for b in range(ray_blocks):
        residual = acc_f[b] - measured_ref[pl.ds(b, 1), :]
        rpad[b, views] = residual.astype(jnp.bfloat16)
    total(adjoint_group, views, back)

    each(1, views, lambda d: b_copy(d, lax.rem(me_v + d, views), me_v).start())
    brecv[me_v] = back[me_v]
    own_gram = dot_t(positions, deviation, lax.Precision.HIGHEST)

    d_all.wait_recv()
    if views <= 16:
        wide = jnp.concatenate([back[v] for v in range(views)], axis=1)
        spread = jnp.concatenate([devs[v] for v in range(views)], axis=1)
        high, low = split_high_low(wide)
        gram = dot_t(high, spread) + dot_t(low, spread)
    else:

        def add(v, gram):
            high, low = split_high_low(back[v])
            return gram + dot_t(high, devs[v]) + dot_t(low, devs[v])

        gram = lax.fori_loop(0, views, add, jnp.zeros((rows, walkers), jnp.float32))
    grecv[me_v] = misfit_weight * gram + own_gram
    each(1, views, lambda d: g_copy(d, me_v).start())
    for sent in (w_all, x_all, d_all, b_all):
        sent.wait_send()

    b_all.wait_recv()
    out_ref[0] = misfit_weight * jnp.sum(brecv[...], axis=0) + positions

    g_all.wait_recv()
    gram = jnp.sum(grecv[...], axis=0)
    step_size = walkers / (4.0 * (voxel_count + 1))
    coefficient = (
        -(step_size / walkers) * gram
        + math.sqrt(2.0 * step_size / walkers) * noise_ref[...]
    )
    moved = jnp.dot(
        coefficient,
        deviation,
        precision=lax.Precision.HIGHEST,
        preferred_element_type=jnp.float32,
    )
    own_deviation = positions - mean
    out_ref[1] = moved + step_size * (voxel_count + 1) / walkers * own_deviation

    g_all.wait_send()


def shards(views, walks, positions, tile_values, tile_rays, tile_voxels, tile_count, measured, langevin_noise):
    rows, tile = positions.shape
    slots = tile_values.shape[0]
    ray_blocks = measured.shape[0] // tile
    walkers = rows * walks
    dma = pltpu.SemaphoreType.DMA
    vmem = pl.BlockSpec(memory_space=pltpu.VMEM)
    hbm = pl.BlockSpec(memory_space=pltpu.HBM)
    both = pl.pallas_call(
        functools.partial(step_kernel, views, walks),
        out_shape=pltpu.VMEM((2, rows, tile), jnp.float32),
        in_specs=[vmem, hbm, hbm, hbm, hbm, hbm, hbm],
        out_specs=vmem,
        scratch_shapes=[
            pltpu.SMEM(tile_rays.shape, jnp.int32),
            pltpu.SMEM(tile_voxels.shape, jnp.int32),
            pltpu.SMEM(tile_count.shape, jnp.int32),
            pltpu.VMEM((ray_blocks, tile), jnp.float32),
            pltpu.VMEM(langevin_noise.shape, jnp.float32),
            dma((5,)),
            pltpu.VMEM((slots, tile, tile), jnp.bfloat16),
            pltpu.VMEM((views, 2 * ray_blocks, rows, tile), jnp.bfloat16),
            pltpu.VMEM((ray_blocks, 2 * views, rows, tile), jnp.bfloat16),
            pltpu.VMEM((walks, rows, tile), jnp.float32),
            pltpu.VMEM((views, walkers, tile), jnp.bfloat16),
            pltpu.VMEM((views, rows, tile), jnp.float32),
            pltpu.VMEM((views, rows, tile), jnp.float32),
            pltpu.VMEM((views, rows, walkers), jnp.float32),
            pltpu.VMEM((ray_blocks, rows, tile), jnp.float32),
            dma((CHUNKS,)),
            dma,
            dma,
            dma,
            dma,
            dma,
            dma,
            dma,
            dma,
            dma,
            dma,
        ],
        compiler_params=pltpu.CompilerParams(
            collective_id=0,
            has_side_effects=True,
            vmem_limit_bytes=56 * 1024 * 1024,
        ),
        cost_estimate=pl.CostEstimate(
            flops=4 * slots * tile * tile * rows,
            bytes_accessed=2 * slots * tile * tile,
            transcendentals=0,
        ),
    )(
        positions,
        tile_values,
        tile_rays,
        tile_voxels,
        tile_count,
        measured.reshape(ray_blocks, tile),
        langevin_noise,
    )
    return both[0], both[1]


def solution(mesh):
    in_specs = (
        P("walk", "view"),
        P("view", None, None),
        P("view"),
        P("view"),
        P("view"),
        P("view"),
        P("walk", None),
    )
    out_specs = (P("walk", "view"), P("walk", "view"))
    body = functools.partial(shards, mesh.shape["view"], mesh.shape["walk"])
    return jax.shard_map(body, mesh=mesh, in_specs=in_specs, out_specs=out_specs, check_vma=False)
```

```python
import functools
import math

import jax
import jax.numpy as jnp
from jax import lax
from jax.experimental import pallas as pl
from jax.experimental.pallas import tpu as pltpu
from jax.sharding import PartitionSpec as P

misfit_weight = 4.0
MESH = pl.DeviceIdType.MESH
GROUP = 8
CHUNKS = 1


def each(start, stop, body):
    if stop - start <= 16:
        for index in range(start, stop):
            body(index)
    else:

        @pl.loop(start, stop)
        def _(index):
            body(index)


def split_high_low(value):
    high = value.astype(jnp.bfloat16)
    low = (value - high.astype(jnp.float32)).astype(jnp.bfloat16)
    return high, low


def dot_t(left, right, precision=None):
    return lax.dot_general(
        left,
        right,
        (((1,), (1,)), ((), ())),
        precision=precision,
        preferred_element_type=jnp.float32,
    )


def step_kernel(
    views,
    walks,
    pos_ref,
    tiles_hbm,
    rays_hbm,
    voxels_hbm,
    count_hbm,
    measured_hbm,
    noise_hbm,
    out_ref,
    rays_ref,
    voxels_ref,
    count_ref,
    measured_ref,
    noise_ref,
    small_sem,
    tiles,
    xpad,
    rpad,
    ens,
    devs,
    back,
    brecv,
    grecv,
    acc_f,
    tile_sem,
    x_send,
    x_recv,
    w_send,
    w_recv,
    d_send,
    d_recv,
    b_send,
    b_recv,
    g_send,
    g_recv,
):
    me_v = lax.axis_index("view")
    me_w = lax.axis_index("walk")
    rows = pos_ref.shape[0]
    slots, tile, _ = tiles.shape
    ray_blocks = measured_ref.shape[0]
    walkers = rows * walks
    voxel_count = views * tile
    chunk = slots // CHUNKS

    barrier = pltpu.get_barrier_semaphore()

    def greet_view(d):
        pl.semaphore_signal(
            barrier,
            inc=1,
            device_id={"view": lax.rem(me_v + d, views)},
            device_id_type=MESH,
        )

    def greet_walk(d):
        pl.semaphore_signal(
            barrier,
            inc=1,
            device_id={"walk": lax.rem(me_w + d, walks)},
            device_id_type=MESH,
        )

    each(1, walks, greet_walk)
    each(1, views, greet_view)

    def tile_copy(c):
        part = pl.ds(c * chunk, chunk)
        return pltpu.make_async_copy(tiles_hbm.at[part], tiles.at[part], tile_sem.at[c])

    small = [
        pltpu.make_async_copy(source, target, small_sem.at[k])
        for k, (source, target) in enumerate(
            (
                (rays_hbm, rays_ref),
                (voxels_hbm, voxels_ref),
                (count_hbm, count_ref),
                (measured_hbm, measured_ref),
                (noise_hbm, noise_ref),
            )
        )
    ]

    positions = pos_ref[...]
    xpad[me_v, ray_blocks] = positions.astype(jnp.bfloat16)
    ens[me_w] = positions

    pl.semaphore_wait(barrier, views + walks - 2)

    def view_copy(d, src, dst, send, recv):
        return pltpu.make_async_remote_copy(
            src_ref=src,
            dst_ref=dst,
            send_sem=send,
            recv_sem=recv,
            device_id={"view": lax.rem(me_v + d, views)},
            device_id_type=MESH,
        )

    def x_copy(d, owner):
        part = xpad.at[owner, ray_blocks]
        return view_copy(d, part, part, x_send, x_recv)

    def w_copy(d, owner):
        return pltpu.make_async_remote_copy(
            src_ref=ens.at[owner],
            dst_ref=ens.at[owner],
            send_sem=w_send,
            recv_sem=w_recv,
            device_id={"walk": lax.rem(me_w + d, walks)},
            device_id_type=MESH,
        )

    def d_copy(d, owner):
        return view_copy(d, devs.at[owner], devs.at[owner], d_send, d_recv)

    def b_copy(d, source, owner):
        return view_copy(d, back.at[source], brecv.at[owner], b_send, b_recv)

    def g_copy(d, owner):
        return view_copy(d, grecv.at[owner], grecv.at[owner], g_send, g_recv)

    def all_views(like, send, recv):
        return view_copy(1, like, like, send, recv)

    peers = pl.ds(0, views - 1)
    x_all = all_views(rpad.at[0, peers], x_send, x_recv)
    d_all = all_views(devs.at[peers], d_send, d_recv)
    b_all = all_views(brecv.at[peers], b_send, b_recv)
    g_all = all_views(grecv.at[peers], g_send, g_recv)
    w_part = ens.at[pl.ds(0, walks - 1)]
    w_all = pltpu.make_async_remote_copy(
        src_ref=w_part,
        dst_ref=w_part,
        send_sem=w_send,
        recv_sem=w_recv,
        device_id={"walk": lax.rem(me_w + 1, walks)},
        device_id_type=MESH,
    )

    each(1, walks, lambda d: w_copy(d, me_w).start())
    each(1, views, lambda d: x_copy(d, me_v).start())
    for copy in small:
        copy.start()
    for c in range(CHUNKS):
        tile_copy(c).start()

    def clear(ref, index, middle):
        size = ref.shape[1]
        after = size - middle - 1
        ref[index, pl.ds(0, middle)] = jnp.zeros((middle, rows, tile), jnp.bfloat16)
        ref[index, pl.ds(middle + 1, after)] = jnp.zeros((after, rows, tile), jnp.bfloat16)

    each(0, views, lambda v: clear(xpad, v, ray_blocks))
    each(0, ray_blocks, lambda b: clear(rpad, b, views))

    w_all.wait_recv()
    ensemble = ens[...].reshape(walkers, tile)
    mean = jnp.sum(ensemble, axis=0, keepdims=True) / walkers
    deviation = ensemble - mean
    devs[me_v] = deviation.astype(jnp.bfloat16)
    each(1, views, lambda d: d_copy(d, me_v).start())

    for copy in small:
        copy.wait()
    live = count_ref[0]

    def is_live(s):
        return jnp.minimum(jnp.maximum(live - s, 0), 1)

    x_all.wait_recv()
    for c in range(CHUNKS):
        tile_copy(c).wait()

    def forward_group(first):
        lefts, rights = [], []
        for k in range(GROUP):
            s = first + k
            start = is_live(s) * (ray_blocks - rays_ref[s])
            window = xpad[voxels_ref[s], pl.ds(start, ray_blocks)]
            lefts.append(window.reshape(ray_blocks * rows, tile))
            rights.append(tiles[s])
        return dot_t(jnp.concatenate(lefts, axis=1), jnp.concatenate(rights, axis=1))

    def adjoint_group(first):
        lefts = []
        for k in range(GROUP):
            s = first + k
            start = is_live(s) * (views - voxels_ref[s])
            window = rpad[rays_ref[s], pl.ds(start, views)]
            lefts.append(window.reshape(views * rows, tile))
        right = tiles[pl.ds(first, GROUP)].reshape(GROUP * tile, tile)
        return jnp.dot(
            jnp.concatenate(lefts, axis=1), right, preferred_element_type=jnp.float32
        )

    def total(group, window, store):
        if window * rows <= 512:
            value = group(0)
            for first in range(GROUP, slots, GROUP):
                value = value + group(first)
            store[...] = value.reshape(store.shape)
        else:
            store[...] = jnp.zeros_like(store)

            @pl.loop(0, slots // GROUP)
            def _(g):
                store[...] += group(g * GROUP).reshape(store.shape)

    total(forward_group, ray_blocks, acc_f)
    for b in range(ray_blocks):
        residual = acc_f[b] - measured_ref[pl.ds(b, 1), :]
        rpad[b, views] = residual.astype(jnp.bfloat16)
    total(adjoint_group, views, back)

    each(1, views, lambda d: b_copy(d, lax.rem(me_v + d, views), me_v).start())
    brecv[me_v] = back[me_v]
    own_gram = dot_t(positions, deviation, lax.Precision.HIGHEST)

    d_all.wait_recv()
    if views <= 16:
        wide = jnp.concatenate([back[v] for v in range(views)], axis=1)
        spread = jnp.concatenate([devs[v] for v in range(views)], axis=1)
        high, low = split_high_low(wide)
        gram = dot_t(high, spread) + dot_t(low, spread)
    else:

        def add(v, gram):
            high, low = split_high_low(back[v])
            return gram + dot_t(high, devs[v]) + dot_t(low, devs[v])

        gram = lax.fori_loop(0, views, add, jnp.zeros((rows, walkers), jnp.float32))
    grecv[me_v] = misfit_weight * gram + own_gram
    each(1, views, lambda d: g_copy(d, me_v).start())
    for sent in (w_all, x_all, d_all, b_all):
        sent.wait_send()

    b_all.wait_recv()
    out_ref[0] = misfit_weight * jnp.sum(brecv[...], axis=0) + positions

    g_all.wait_recv()
    gram = jnp.sum(grecv[...], axis=0)
    step_size = walkers / (4.0 * (voxel_count + 1))
    coefficient = (
        -(step_size / walkers) * gram
        + math.sqrt(2.0 * step_size / walkers) * noise_ref[...]
    )
    moved = jnp.dot(
        coefficient,
        deviation,
        precision=lax.Precision.HIGHEST,
        preferred_element_type=jnp.float32,
    )
    own_deviation = positions - mean
    out_ref[1] = moved + step_size * (voxel_count + 1) / walkers * own_deviation

    g_all.wait_send()


def shards(views, walks, positions, tile_values, tile_rays, tile_voxels, tile_count, measured, langevin_noise):
    rows, tile = positions.shape
    slots = tile_values.shape[0]
    ray_blocks = measured.shape[0] // tile
    walkers = rows * walks
    dma = pltpu.SemaphoreType.DMA
    vmem = pl.BlockSpec(memory_space=pltpu.VMEM)
    hbm = pl.BlockSpec(memory_space=pltpu.HBM)
    both = pl.pallas_call(
        functools.partial(step_kernel, views, walks),
        out_shape=pltpu.VMEM((2, rows, tile), jnp.float32),
        in_specs=[vmem, hbm, hbm, hbm, hbm, hbm, hbm],
        out_specs=vmem,
        scratch_shapes=[
            pltpu.SMEM(tile_rays.shape, jnp.int32),
            pltpu.SMEM(tile_voxels.shape, jnp.int32),
            pltpu.SMEM(tile_count.shape, jnp.int32),
            pltpu.VMEM((ray_blocks, tile), jnp.float32),
            pltpu.VMEM(langevin_noise.shape, jnp.float32),
            dma((5,)),
            pltpu.VMEM((slots, tile, tile), jnp.bfloat16),
            pltpu.VMEM((views, 2 * ray_blocks, rows, tile), jnp.bfloat16),
            pltpu.VMEM((ray_blocks, 2 * views, rows, tile), jnp.bfloat16),
            pltpu.VMEM((walks, rows, tile), jnp.float32),
            pltpu.VMEM((views, walkers, tile), jnp.bfloat16),
            pltpu.VMEM((views, rows, tile), jnp.float32),
            pltpu.VMEM((views, rows, tile), jnp.float32),
            pltpu.VMEM((views, rows, walkers), jnp.float32),
            pltpu.VMEM((ray_blocks, rows, tile), jnp.float32),
            dma((CHUNKS,)),
            dma,
            dma,
            dma,
            dma,
            dma,
            dma,
            dma,
            dma,
            dma,
            dma,
        ],
        compiler_params=pltpu.CompilerParams(
            collective_id=0,
            has_side_effects=True,
            vmem_limit_bytes=56 * 1024 * 1024,
        ),
        cost_estimate=pl.CostEstimate(
            flops=4 * slots * tile * tile * rows,
            bytes_accessed=2 * slots * tile * tile,
            transcendentals=0,
        ),
    )(
        positions,
        tile_values,
        tile_rays,
        tile_voxels,
        tile_count,
        measured.reshape(ray_blocks, tile),
        langevin_noise,
    )
    return both[0], both[1]


def solution(mesh):
    in_specs = (
        P("walk", "view"),
        P("view", None, None),
        P("view"),
        P("view"),
        P("view"),
        P("view"),
        P("walk", None),
    )
    out_specs = (P("walk", "view"), P("walk", "view"))
    body = functools.partial(shards, mesh.shape["view"], mesh.shape["walk"])
    return jax.shard_map(body, mesh=mesh, in_specs=in_specs, out_specs=out_specs, check_vma=False)
```
